256 devices in a mesh: frame: 32 (over y, z_lo, x), head: 8 (over z_hi, core).
Axes of the slice: x: 4, y: 4, z: 8 (z_hi: 4, z_lo: 2; z = z_hi * 2 + z_lo), core: 2. Of those that a mesh axis runs over, the one named last changes fastest.
Arguments:
- queries: bfloat16 [65536, 2048], P(('frame', 'head')), may hold values from -32 to 32
- keys: bfloat16 [65536, 2048], P(('frame', 'head')), may hold values from -32 to 32
- values: bfloat16 [65536, 2048], P(('frame', 'head')), may hold values from -6 to 6
- windows: int32 [512, 27], P('frame'), may hold values from 0 to 511, as said below
- counts: int32 [512], replicated, may hold values from 48 to 128
Outputs:
- attended: bfloat16 [65536, 2048], P(('frame', 'head'))
The draws below stay inside these ranges and needn't reach their ends.
Inputs may be any that keep to these rules, and one draw needn't show every extreme that they name: `windows`: row t lists tile t first, then 27 - 1 other distinct tiles whose frame pair (tile // 16) differs from that of tile t by at most one.
All inputs are finite; a program needn't handle non-finite values.
Results may differ from the reference program's by a relative error of at most 0.01.
Values may be sent and summed in bfloat16 or wider, within the bound.
A program may use at most 128 MiB of HBM per device.

```python
import jax
import jax.numpy as jnp
from jax import lax

HEADS = 16
HEAD_DIM = 128
TILE = 128
WIN = 27
TL = 16
WIDTH = 2048
NTILES = 512
TOKENS = 65536


def paired_fields(key):
    grid_shape = (NTILES, TILE, HEADS, HEAD_DIM)
    base_q = jnp.clip(jax.random.normal(jax.random.fold_in(key, 11), grid_shape, jnp.float32), -4.0, 4.0)
    base_k = jnp.clip(jax.random.normal(jax.random.fold_in(key, 12), grid_shape, jnp.float32), -4.0, 4.0)
    return (base_q.reshape(NTILES * TILE, HEADS * HEAD_DIM), base_k.reshape(NTILES * TILE, HEADS * HEAD_DIM))


def draw_queries(key, part):
    return paired_fields(key)[0].astype(jnp.bfloat16)


def draw_keys(key, part):
    return paired_fields(key)[1].astype(jnp.bfloat16)


def draw_windows(key, part):
    tile_ids = jnp.arange(NTILES, dtype=jnp.int32)
    offsets = jnp.arange(3 * TL, dtype=jnp.int32)
    layer_of = tile_ids // TL
    candidates = (layer_of[:, None] - 1) * TL + offsets[None, :]
    allowed = (candidates >= 0) & (candidates < NTILES) & (candidates != tile_ids[:, None])
    random_part = jax.random.randint(jax.random.fold_in(key, 21), (NTILES, 3 * TL), 0, 2 ** 20)
    tile_ranking = jnp.where(allowed, random_part * 256 + offsets[None, :], 2 ** 30)
    ordering = jnp.argsort(tile_ranking, axis=-1, stable=True)[:, :WIN - 1]
    picked = jnp.take_along_axis(candidates, ordering, axis=-1)
    return jnp.concatenate([tile_ids[:, None], picked], axis=1).astype(jnp.int32)


def draw_counts(key, part):
    lowest = TILE * 3 // 8
    ragged = jax.random.randint(jax.random.fold_in(key, 31), (NTILES,), lowest, TILE + 1)
    filled = jax.random.randint(jax.random.fold_in(key, 32), (NTILES,), 0, 2) == 0
    result = jnp.where(filled, TILE, ragged).astype(jnp.int32)
    full_at = jax.random.randint(jax.random.fold_in(key, 33), (), 0, NTILES)
    thin_at = (full_at + 1 + jax.random.randint(jax.random.fold_in(key, 34), (), 0, NTILES - 1)) % NTILES
    result = result.at[full_at].set(TILE)
    result = result.at[thin_at].set(lowest)
    return result.astype(jnp.int32)


def steps_of(rng, shape, cuts, smallest, top_value):
    level = 1.0
    for axis_at, blocks in cuts:
        heights = jax.random.uniform(jax.random.fold_in(jax.random.fold_in(rng, 6), axis_at), (blocks,), jnp.float32, smallest / len(cuts), top_value / len(cuts))
        level = level * jnp.repeat(jnp.exp(heights), shape[axis_at] // blocks).reshape((-1,) + (1,) * (len(shape) - 1 - axis_at))
    return level


def noise(stream_key, extent, scale, limit, split=(), kind=jnp.bfloat16):
    loudness = steps_of(stream_key, extent, split, -0.22, 0.18) if split else 1.0
    drawn = jax.random.normal(stream_key, extent, jnp.float32) * scale * loudness
    return jnp.minimum(jnp.maximum(drawn, -limit), limit).astype(kind)


def setup_inputs(seed: int = 0) -> dict:
    seeds = jax.random.split(jax.random.key(seed), 6)
    return {
        "queries": draw_queries(jax.random.fold_in(seeds[5], 71), 0),
        "keys": draw_keys(jax.random.fold_in(seeds[5], 71), 0),
        "values": noise(seeds[2], (TOKENS, WIDTH), 1.0, 6.0, ((0, 256),)),
        "windows": draw_windows(jax.random.fold_in(seeds[5], 71), 0),
        "counts": draw_counts(jax.random.fold_in(seeds[5], 71), 0),
    }


def reference(queries, keys, values, windows, counts):
    score_scale = HEAD_DIM ** -0.5
    q_tiles = queries.reshape(-1, TILE, HEADS, HEAD_DIM)
    k_tiles = keys.reshape(-1, TILE, HEADS, HEAD_DIM)
    v_tiles = values.reshape(-1, TILE, HEADS, HEAD_DIM)
    positions = jnp.arange(TILE, dtype=jnp.int32)

    def one_tile(inputs):
        q_rows, window_row = inputs
        k_rows = k_tiles[window_row].reshape(-1, HEADS, HEAD_DIM).astype(jnp.float32)
        v_rows = v_tiles[window_row].reshape(-1, HEADS, HEAD_DIM).astype(jnp.float32)
        usable = (positions[None, :] < counts[window_row][:, None]).reshape(-1)
        scores = jnp.einsum("qhd,khd->hqk", q_rows.astype(jnp.float32), k_rows) * score_scale
        scores = jnp.where(usable[None, None, :], scores, -1e30)
        highest = jnp.max(scores, axis=-1, keepdims=True)
        attention_weights = jnp.exp(scores - highest).astype(jnp.bfloat16)
        totals = jnp.sum(attention_weights.astype(jnp.float32), axis=-1, keepdims=True)
        mixed_values = jnp.einsum("hqk,khd->hqd", attention_weights.astype(jnp.float32), v_rows) / totals
        return jnp.transpose(mixed_values, (1, 0, 2)).reshape(TILE, HEADS * HEAD_DIM).astype(jnp.bfloat16)

    result = lax.map(one_tile, (q_tiles, windows))
    return result.reshape(-1, HEADS * HEAD_DIM)
```

```python
import math

import jax
import jax.numpy as jnp
from jax import lax
from jax.experimental import pallas as pl
from jax.experimental.pallas import tpu as pltpu
from jax.sharding import PartitionSpec as P

HEADS = 16
DIM = 128
TILE = 128
WIN = 27
TL = 16
PEERS = 16
ROWS = 256
SCALE = math.log2(math.e) / math.sqrt(DIM)
MESH = pl.DeviceIdType.MESH


def div(a, b):
    return lax.div(a, jnp.int32(b))


def rem(a, b):
    return lax.rem(a, jnp.int32(b))


def owner(pair, head):
    z, b = div(head, 2), rem(head, 2)
    zh = div(z, 2)
    x = 2 * b + rem(div(pair, 2) + div(pair, 4) + zh, 2)
    return (div(pair, 4) * 2 + rem(z, 2)) * 4 + x, zh * 2 + rem(pair, 2)


def spread(k):
    return div(k + 1, 2) * (2 * rem(k, 2) - 1)


def kernel(
    q_ref, k_ref, v_ref, win_ref, counts_hbm, out_ref,
    qbuf, kraw, vraw, keys, vals, obuf, scores, wdst, wsm, counts_ref,
    in_send, in_recv, halo_send, halo_recv, o_send, o_recv, w_send, w_recv, local,
):
    f, hi = lax.axis_index("frame"), lax.axis_index("head")
    zl, x = rem(div(f, 4), 2), rem(f, 4)
    zh, core = div(hi, 2), rem(hi, 2)
    src_pair = div(f, 2)
    my_slot = rem(f, 2) * 8 + hi
    my_z = zh * 2 + zl
    head = 2 * my_z + div(x, 2)
    pair = div(f, 8) * 4 + rem(x + zh + div(f, 8), 2) * 2 + core
    last_pair = lax.axis_size("frame") // 2 - 1
    has_left, has_right = pair > 0, pair < last_pair
    left = owner(jnp.maximum(pair - 1, 0), head)
    right = owner(jnp.minimum(pair + 1, last_pair), head)

    def is_me(dev):
        return (dev[0] == f) & (dev[1] == hi)

    sign = 1 - 2 * core

    def dest_head(i, side):
        z = rem(my_z + side * spread(div(i, 2)) + 8, 8)
        return 2 * z + rem(i, 2)

    def source_slot(i):
        r = rem(i, 4)
        z = rem(zh + sign * spread(div(i, 4)) + 4, 4)
        return rem(r, 2) * 8 + z * 2 + div(r, 2)

    def source_dev(slot):
        return 2 * pair + div(slot, 8), rem(slot, 8)

    barrier = pltpu.get_barrier_semaphore()

    def greet(dev, when):
        @pl.when(when)
        def _():
            pl.semaphore_signal(barrier, inc=1, device_id=dev, device_id_type=MESH)

    def greet_step(i, carry):
        src = source_dev(i)
        greet(src, jnp.logical_not(is_me(src)))
        return carry

    counts_copy = pltpu.make_async_copy(counts_hbm, counts_ref, local.at[0])
    counts_copy.start()
    lax.fori_loop(0, PEERS, greet_step, 0)
    greet(left, has_left)
    greet(right, has_right)
    selfish = (div(f, 2) == pair).astype(jnp.int32)
    pl.semaphore_wait(
        barrier, 16 - selfish + has_left.astype(jnp.int32) + has_right.astype(jnp.int32)
    )

    def send(a, src_ref, dst_ref, h):
        dst = owner(src_pair, h)
        src = src_ref.at[:, pl.ds(pl.multiple_of(h * DIM, DIM), DIM)]
        mine = is_me(dst)

        @pl.when(jnp.logical_not(mine))
        def _():
            pltpu.make_async_remote_copy(
                src_ref=src, dst_ref=dst_ref, send_sem=in_send.at[a, h],
                recv_sem=in_recv.at[a, my_slot], device_id=dst, device_id_type=MESH,
            ).start()

        @pl.when(mine)
        def _():
            pltpu.make_async_copy(src, dst_ref, in_recv.at[a, my_slot]).start()

    def sends(i, carry):
        send(0, k_ref, kraw.at[8 + my_slot], dest_head(i, sign))
        send(1, v_ref, vraw.at[8 + my_slot], dest_head(i, -sign))
        return carry

    def window_send(b, start):
        h = 2 * hi + b
        dst = owner(src_pair, h)
        mine = is_me(dst)
        there = wdst.at[rem(f, 2)]

        @pl.when(jnp.logical_not(mine))
        def _():
            copy = pltpu.make_async_remote_copy(
                src_ref=win_ref, dst_ref=there, send_sem=w_send.at[b],
                recv_sem=w_recv.at[rem(f, 2)], device_id=dst, device_id_type=MESH,
            )
            if start:
                copy.start()
            else:
                copy.wait_send()

        if start:

            @pl.when(mine)
            def _():
                pltpu.make_async_copy(win_ref, there, w_recv.at[rem(f, 2)]).start()

    for b in range(2):
        window_send(b, True)
    lax.fori_loop(0, PEERS, sends, 0)

    first_tile = (2 * pair - 1) * TL
    row_ids = lax.broadcasted_iota(jnp.int32, (TILE, DIM), 0)

    def prepare(r):
        for u in range(2):
            count = counts_ref[first_tile + 2 * r + u]
            usable = row_ids < count
            k = kraw[r, u * TILE : (u + 1) * TILE, :].astype(jnp.float32)
            keys[2 * r + u] = jnp.where(usable, k, k[0:1, :]).astype(jnp.bfloat16)
            v = vraw[r, u * TILE : (u + 1) * TILE, :].astype(jnp.float32)
            vals[2 * r + u, :, 0:DIM] = jnp.where(usable, v, 0.0).astype(jnp.bfloat16)
            vals[2 * r + u, :, DIM : 2 * DIM] = jnp.where(usable, 1.0, 0.0).astype(jnp.bfloat16)

    def halo(a, raw, slot, dev, there):
        return pltpu.make_async_remote_copy(
            src_ref=raw.at[8 + slot], dst_ref=raw.at[there], send_sem=halo_send.at[a, slot],
            recv_sem=halo_recv.at[a, slot], device_id=dev, device_id_type=MESH,
        )

    def arrivals(i, carry):
        slot = source_slot(i)
        for a, raw in ((0, kraw), (1, vraw)):
            here = raw.at[8 + slot]
            pltpu.make_async_copy(here, here, in_recv.at[a, slot]).wait()

            @pl.when((slot < 8) & has_left)
            def _():
                halo(a, raw, slot, left, 24 + rem(slot, 8)).start()

            @pl.when((slot >= 8) & has_right)
            def _():
                halo(a, raw, slot, right, rem(slot, 8)).start()

        send(2, q_ref, qbuf.at[my_slot], dest_head(i, sign))
        prepare(8 + slot)
        return carry

    counts_copy.wait()
    lax.fori_loop(0, PEERS, arrivals, 0)

    def halo_arrivals(i, carry):
        slot = source_slot(i)
        from_left = slot >= 8
        r = lax.select(from_left, rem(slot, 8), 24 + rem(slot, 8))

        @pl.when((from_left & has_left) | (jnp.logical_not(from_left) & has_right))
        def _():
            for a, raw in ((0, kraw), (1, vraw)):
                here = raw.at[r]
                pltpu.make_async_copy(here, here, halo_recv.at[a, slot]).wait()
            prepare(r)

        return carry

    for half in range(2):
        here = wdst.at[half]
        pltpu.make_async_copy(here, here, w_recv.at[half]).wait()
    copy = pltpu.make_async_copy(wdst, wsm, local.at[1])
    copy.start()
    copy.wait()
    lax.fori_loop(0, PEERS, halo_arrivals, 0)

    def attend(slot, u):
        q = qbuf[slot, u * TILE : (u + 1) * TILE, :]
        half, row = div(slot, 8), 2 * rem(slot, 8) + u
        at = [jnp.clip(wsm[half, row, j] - first_tile, 0, 4 * TL - 1) for j in range(WIN)]
        highest = None
        for j in range(0, WIN, 2):
            k = keys[at[j]]
            if j + 1 < WIN:
                k = jnp.concatenate([k, keys[at[j + 1]]], axis=0)
            s = lax.dot_general(q, k, (((1,), (1,)), ((), ())), preferred_element_type=jnp.float32)
            scores[u, :, j * TILE : j * TILE + k.shape[0]] = s
            for part in range(k.shape[0] // TILE):
                block = s[:, part * TILE : (part + 1) * TILE]
                highest = block if highest is None else jnp.maximum(highest, block)
        highest = jnp.max(highest, axis=1, keepdims=True)
        total = jnp.zeros((TILE, 2 * DIM), jnp.float32)
        for j in range(0, WIN, 2):
            v = vals[at[j]]
            if j + 1 < WIN:
                v = jnp.concatenate([v, vals[at[j + 1]]], axis=0)
            s = scores[u, :, j * TILE : j * TILE + v.shape[0]]
            weights = jnp.exp2((s - highest) * SCALE).astype(jnp.bfloat16)
            total += jnp.dot(weights, v, preferred_element_type=jnp.float32)
        result = total[:, :DIM] / total[:, DIM:]
        obuf[slot, u * TILE : (u + 1) * TILE, :] = result.astype(jnp.bfloat16)

    columns = pl.ds(pl.multiple_of(head * DIM, DIM), DIM)

    def result_copy(slot, dev):
        return pltpu.make_async_remote_copy(
            src_ref=obuf.at[slot], dst_ref=out_ref.at[:, columns], send_sem=o_send.at[slot],
            recv_sem=o_recv.at[head], device_id=dev, device_id_type=MESH,
        )

    def compute(i, carry):
        slot = source_slot(i)
        here = qbuf.at[slot]
        pltpu.make_async_copy(here, here, in_recv.at[2, slot]).wait()
        for u in range(2):
            attend(slot, u)
        dev = source_dev(slot)
        mine = is_me(dev)

        @pl.when(jnp.logical_not(mine))
        def _():
            result_copy(slot, dev).start()

        @pl.when(mine)
        def _():
            pltpu.make_async_copy(obuf.at[slot], out_ref.at[:, columns], o_recv.at[head]).start()

        return carry

    lax.fori_loop(0, PEERS, compute, 0)

    def finish(i, carry):
        dst = owner(src_pair, i)

        @pl.when(jnp.logical_not(is_me(dst)))
        def _():
            for a, ref in ((0, k_ref), (1, v_ref), (2, q_ref)):
                src = ref.at[:, pl.ds(pl.multiple_of(i * DIM, DIM), DIM)]
                pltpu.make_async_copy(src, src, in_send.at[a, i]).wait()

        @pl.when(((i < 8) & has_left) | ((i >= 8) & has_right))
        def _():
            for a, raw in ((0, kraw), (1, vraw)):
                there = raw.at[8 + i]
                pltpu.make_async_copy(there, there, halo_send.at[a, i]).wait()

        @pl.when(jnp.logical_not(is_me(source_dev(i))))
        def _():
            pltpu.make_async_copy(obuf.at[i], obuf.at[i], o_send.at[i]).wait()

        got = out_ref.at[:, pl.ds(pl.multiple_of(i * DIM, DIM), DIM)]
        pltpu.make_async_copy(got, got, o_recv.at[i]).wait()
        return carry

    lax.fori_loop(0, PEERS, finish, 0)
    for b in range(2):
        window_send(b, False)


def shards(queries, keys, values, windows, counts):
    anywhere = pl.BlockSpec(memory_space=pltpu.HBM)
    dma = pltpu.SemaphoreType.DMA
    return pl.pallas_call(
        kernel,
        out_shape=jax.ShapeDtypeStruct(queries.shape, jnp.bfloat16),
        in_specs=[
            anywhere,
            anywhere,
            anywhere,
            anywhere,
            anywhere,
        ],
        out_specs=anywhere,
        scratch_shapes=[
            pltpu.VMEM((PEERS, ROWS, DIM), jnp.bfloat16),
            pltpu.VMEM((2 * PEERS, ROWS, DIM), jnp.bfloat16),
            pltpu.VMEM((2 * PEERS, ROWS, DIM), jnp.bfloat16),
            pltpu.VMEM((4 * TL, TILE, DIM), jnp.bfloat16),
            pltpu.VMEM((4 * TL, TILE, 2 * DIM), jnp.bfloat16),
            pltpu.VMEM((PEERS, ROWS, DIM), jnp.bfloat16),
            pltpu.VMEM((2, TILE, WIN * TILE), jnp.float32),
            pltpu.VMEM((2, TL, WIN), jnp.int32),
            pltpu.SMEM((2, TL, WIN), jnp.int32),
            pltpu.SMEM((32 * TL,), jnp.int32),
            dma((3, PEERS)),
            dma((3, PEERS)),
            dma((2, PEERS)),
            dma((2, PEERS)),
            dma((PEERS,)),
            dma((PEERS,)),
            dma((2,)),
            dma((2,)),
            dma((2,)),
        ],
        compiler_params=pltpu.CompilerParams(
            collective_id=0, has_side_effects=True, vmem_limit_bytes=48 * 1024 * 1024
        ),
        name="tile_attention",
    )(queries, keys, values, windows, counts)


def solution(mesh):
    tokens = P(("frame", "head"), None)
    return jax.shard_map(
        shards,
        mesh=mesh,
        in_specs=(tokens, tokens, tokens, P("frame", None), P()),
        out_specs=tokens,
        check_vma=False,
    )
```

```python
import math

import jax
import jax.numpy as jnp
from jax import lax
from jax.experimental import pallas as pl
from jax.experimental.pallas import tpu as pltpu
from jax.sharding import PartitionSpec as P

HEADS = 16
DIM = 128
TILE = 128
WIN = 27
TL = 16
PEERS = 16
ROWS = 256
PART = 5
SCALE = math.log2(math.e) / math.sqrt(DIM)
KFAR, QFAR = True, False
MESH = pl.DeviceIdType.MESH


def div(a, b):
    return lax.div(a, jnp.int32(b))


def rem(a, b):
    return lax.rem(a, jnp.int32(b))


def owner(pair, head):
    z, b = div(head, 2), rem(head, 2)
    zh = div(z, 2)
    x = 2 * b + rem(div(pair, 2) + div(pair, 4) + zh, 2)
    return (div(pair, 4) * 2 + rem(z, 2)) * 4 + x, zh * 2 + rem(pair, 2)


def spread(k):
    return div(k + 1, 2) * (2 * rem(k, 2) - 1)


def kernel(
    q_ref, k_ref, v_ref, win_ref, counts_hbm, out_ref,
    qbuf, kraw, vraw, keys, vals, obuf, scores, wdst, wsm, counts_ref,
    in_send, in_recv, halo_send, halo_recv, o_send, o_recv, w_send, w_recv, local,
):
    f, hi = lax.axis_index("frame"), lax.axis_index("head")
    zl, x = rem(div(f, 4), 2), rem(f, 4)
    zh, core = div(hi, 2), rem(hi, 2)
    src_pair = div(f, 2)
    my_slot = rem(f, 2) * 8 + hi
    my_z = zh * 2 + zl
    head = 2 * my_z + div(x, 2)
    pair = div(f, 8) * 4 + rem(x + zh + div(f, 8), 2) * 2 + core
    last_pair = lax.axis_size("frame") // 2 - 1
    has_left, has_right = pair > 0, pair < last_pair
    left = owner(jnp.maximum(pair - 1, 0), head)
    right = owner(jnp.minimum(pair + 1, last_pair), head)

    def is_me(dev):
        return (dev[0] == f) & (dev[1] == hi)

    sign = 1 - 2 * core

    def dest_head(i, side, far):
        k = div(i, 2)
        z = rem(my_z + side * spread(7 - k if far else k) + 8, 8)
        return 2 * z + rem(i, 2)

    apart = rem(rem(div(pair, 2), 2) + zl, 2)
    turn = apart * (2 * zl - 1) + (1 - apart) * sign

    def source_slot(i, far):
        r = rem(i, 4)
        k = div(i, 4)
        z = rem(zh + turn * spread(3 - k if far else k) + 4, 4)
        return rem(r, 2) * 8 + z * 2 + div(r, 2)

    def source_dev(slot):
        return 2 * pair + div(slot, 8), rem(slot, 8)

    barrier = pltpu.get_barrier_semaphore()

    def greet(dev, when):
        @pl.when(when)
        def _():
            pl.semaphore_signal(barrier, inc=1, device_id=dev, device_id_type=MESH)

    def greet_step(i, carry):
        src = source_dev(i)
        greet(src, jnp.logical_not(is_me(src)))
        return carry

    counts_copy = pltpu.make_async_copy(counts_hbm, counts_ref, local.at[0])
    counts_copy.start()
    lax.fori_loop(0, PEERS, greet_step, 0)
    greet(left, has_left)
    greet(right, has_right)
    selfish = (div(f, 2) == pair).astype(jnp.int32)
    pl.semaphore_wait(
        barrier, 16 - selfish + has_left.astype(jnp.int32) + has_right.astype(jnp.int32)
    )

    def send(a, src_ref, dst_ref, h):
        dst = owner(src_pair, h)
        src = src_ref.at[:, pl.ds(pl.multiple_of(h * DIM, DIM), DIM)]
        mine = is_me(dst)

        @pl.when(jnp.logical_not(mine))
        def _():
            pltpu.make_async_remote_copy(
                src_ref=src, dst_ref=dst_ref, send_sem=in_send.at[a, h],
                recv_sem=in_recv.at[a, my_slot], device_id=dst, device_id_type=MESH,
            ).start()

        @pl.when(mine)
        def _():
            pltpu.make_async_copy(src, dst_ref, in_recv.at[a, my_slot]).start()

    def sends(i, carry):
        send(0, k_ref, kraw.at[8 + my_slot], dest_head(i, sign, KFAR))
        send(1, v_ref, vraw.at[8 + my_slot], dest_head(i, -sign, KFAR))
        return carry

    def window_send(b, start):
        h = 2 * hi + b
        dst = owner(src_pair, h)
        mine = is_me(dst)
        there = wdst.at[rem(f, 2)]

        @pl.when(jnp.logical_not(mine))
        def _():
            copy = pltpu.make_async_remote_copy(
                src_ref=win_ref, dst_ref=there, send_sem=w_send.at[b],
                recv_sem=w_recv.at[rem(f, 2)], device_id=dst, device_id_type=MESH,
            )
            if start:
                copy.start()
            else:
                copy.wait_send()

        if start:

            @pl.when(mine)
            def _():
                pltpu.make_async_copy(win_ref, there, w_recv.at[rem(f, 2)]).start()

    for b in range(2):
        window_send(b, True)
    lax.fori_loop(0, PEERS, sends, 0)

    first_tile = (2 * pair - 1) * TL
    slots = lax.broadcasted_iota(jnp.int32, (16, TILE), 1)
    row_ids = lax.broadcasted_iota(jnp.int32, (TILE, DIM), 0)

    def prepare(r):
        for u in range(2):
            count = counts_ref[first_tile + 2 * r + u]
            usable = row_ids < count
            k = kraw[r, u * TILE : (u + 1) * TILE, :].astype(jnp.float32)
            keys[2 * r + u] = jnp.where(usable, k, k[0:1, :]).astype(jnp.bfloat16)
            v = vraw[r, u * TILE : (u + 1) * TILE, :].astype(jnp.float32)
            vals[2 * r + u, 0:DIM, :] = jnp.where(usable, v, 0.0).T.astype(jnp.bfloat16)
            vals[2 * r + u, DIM:, :] = jnp.where(slots < count, 1.0, 0.0).astype(jnp.bfloat16)

    def halo(a, raw, slot, dev, there):
        return pltpu.make_async_remote_copy(
            src_ref=raw.at[8 + slot], dst_ref=raw.at[there], send_sem=halo_send.at[a, slot],
            recv_sem=halo_recv.at[a, slot], device_id=dev, device_id_type=MESH,
        )

    def arrivals(i, carry):
        slot = source_slot(i, KFAR)
        for a, raw in ((0, kraw), (1, vraw)):
            here = raw.at[8 + slot]
            pltpu.make_async_copy(here, here, in_recv.at[a, slot]).wait()

            @pl.when((slot < 8) & has_left)
            def _():
                halo(a, raw, slot, left, 24 + rem(slot, 8)).start()

            @pl.when((slot >= 8) & has_right)
            def _():
                halo(a, raw, slot, right, rem(slot, 8)).start()


        @pl.when(i >= 8)
        def _():
            for n in range(2):
                send(2, q_ref, qbuf.at[my_slot], dest_head((i - 8) * 2 + n, sign, QFAR))

        prepare(8 + slot)
        return carry

    for half in range(2):
        here = wdst.at[half]
        pltpu.make_async_copy(here, here, w_recv.at[half]).wait()
    copy = pltpu.make_async_copy(wdst, wsm, local.at[1])
    copy.start()
    copy.wait()

    def place_row(i, carry):
        half, row = div(i, TL), rem(i, TL)
        for j in range(WIN):
            wsm[half, row, j] = jnp.clip(wsm[half, row, j] - first_tile, 0, 4 * TL - 1)
        return carry

    lax.fori_loop(0, 2 * TL, place_row, 0)
    counts_copy.wait()
    lax.fori_loop(0, PEERS, arrivals, 0)

    def halo_arrivals(i, carry):
        slot = source_slot(i, KFAR)
        from_left = slot >= 8
        r = lax.select(from_left, rem(slot, 8), 24 + rem(slot, 8))

        @pl.when((from_left & has_left) | (jnp.logical_not(from_left) & has_right))
        def _():
            for a, raw in ((0, kraw), (1, vraw)):
                here = raw.at[r]
                pltpu.make_async_copy(here, here, halo_recv.at[a, slot]).wait()
            prepare(r)

        return carry

    lax.fori_loop(0, PEERS, halo_arrivals, 0)

    def places(slot):
        half, row = div(slot, 8), 2 * rem(slot, 8)
        return [[wsm[half, row + u, j] for j in range(WIN)] for u in range(2)]

    def both(slot):
        q = [qbuf[slot, u * TILE : (u + 1) * TILE, :] for u in range(2)]
        none = jnp.zeros_like(q[0])
        return jnp.concatenate(
            [jnp.concatenate([q[0], none], axis=1), jnp.concatenate([none, q[1]], axis=1)], axis=0
        )

    def score_part(j, queries, at, b, highest):
        n = min(PART, WIN - j)
        k = jnp.concatenate(
            [jnp.concatenate([keys[at[0][j + i]], keys[at[1][j + i]]], axis=1) for i in range(n)], axis=0
        )
        s = lax.dot_general(k, queries, (((1,), (1,)), ((), ())), preferred_element_type=jnp.float32)
        scores[b, j * TILE : (j + n) * TILE, :] = s
        part = jnp.max(s.reshape(n * TILE // 8, 8, 2 * TILE), axis=0)
        return part if highest is None else jnp.maximum(highest, part)

    def value_part(j, u, at, b, highest, total):
        n = min(2, WIN - j)
        v = [vals[at[u][j + i]] for i in range(n)]
        v = v[0] if n == 1 else jnp.concatenate(v, axis=1)
        columns = slice(u * TILE, (u + 1) * TILE)
        s = scores[b, j * TILE : (j + n) * TILE, columns]
        weights = jnp.exp2((s - highest[:, columns]) * SCALE).astype(jnp.bfloat16)
        part = jnp.dot(v, weights, preferred_element_type=jnp.float32)
        return part if total is None else total + part

    def stage(now, then, b, highest):
        at_now, at_then = places(now), places(then)
        queries = both(then)
        parts = list(range(0, WIN, PART))
        steps = [(u, j) for u in range(2) for j in range(0, WIN, 2)]
        coming, done = None, 0
        for step, (u, j) in enumerate(steps):
            if done < len(parts) and done * len(steps) <= step * len(parts):
                coming = score_part(parts[done], queries, at_then, 1 - b, coming)
                done += 1
            total = value_part(j, u, at_now, b, highest, total if j else None)
            if j + 2 > WIN:
                result = total[:DIM] / total[DIM : DIM + 1]
                obuf[now, u * TILE : (u + 1) * TILE, :] = result.T.astype(jnp.bfloat16)
        return jnp.max(coming, axis=0, keepdims=True)

    def query_arrival(slot):
        here = qbuf.at[slot]
        pltpu.make_async_copy(here, here, in_recv.at[2, slot]).wait()

    columns = pl.ds(pl.multiple_of(head * DIM, DIM), DIM)

    def result_copy(slot, dev):
        return pltpu.make_async_remote_copy(
            src_ref=obuf.at[slot], dst_ref=out_ref.at[:, columns], send_sem=o_send.at[slot],
            recv_sem=o_recv.at[head], device_id=dev, device_id_type=MESH,
        )

    def chunk(i, b, highest):
        slot = source_slot(i, QFAR)
        later = jnp.minimum(i + 1, PEERS - 1)
        next_slot = source_slot(later, QFAR)

        @pl.when(later > i)
        def _():
            query_arrival(next_slot)

        highest = stage(slot, next_slot, b, highest)
        dev = source_dev(slot)
        mine = is_me(dev)

        @pl.when(jnp.logical_not(mine))
        def _():
            result_copy(slot, dev).start()

        @pl.when(mine)
        def _():
            pltpu.make_async_copy(obuf.at[slot], out_ref.at[:, columns], o_recv.at[head]).start()

        return highest

    def chunks(i, highest):
        for b in range(2):
            highest = chunk(2 * i + b, b, highest)
        return highest

    first = source_slot(jnp.int32(0), QFAR)
    query_arrival(first)
    highest = None
    for j in range(0, WIN, PART):
        highest = score_part(j, both(first), places(first), 0, highest)
    lax.fori_loop(0, PEERS // 2, chunks, jnp.max(highest, axis=0, keepdims=True))

    def finish(i, carry):
        dst = owner(src_pair, i)

        @pl.when(jnp.logical_not(is_me(dst)))
        def _():
            for a, ref in ((0, k_ref), (1, v_ref), (2, q_ref)):
                src = ref.at[:, pl.ds(pl.multiple_of(i * DIM, DIM), DIM)]
                pltpu.make_async_copy(src, src, in_send.at[a, i]).wait()

        @pl.when(((i < 8) & has_left) | ((i >= 8) & has_right))
        def _():
            for a, raw in ((0, kraw), (1, vraw)):
                there = raw.at[8 + i]
                pltpu.make_async_copy(there, there, halo_send.at[a, i]).wait()

        @pl.when(jnp.logical_not(is_me(source_dev(i))))
        def _():
            pltpu.make_async_copy(obuf.at[i], obuf.at[i], o_send.at[i]).wait()

        got = out_ref.at[:, pl.ds(pl.multiple_of(i * DIM, DIM), DIM)]
        pltpu.make_async_copy(got, got, o_recv.at[i]).wait()
        return carry

    lax.fori_loop(0, PEERS, finish, 0)
    for b in range(2):
        window_send(b, False)


def shards(queries, keys, values, windows, counts):
    anywhere = pl.BlockSpec(memory_space=pltpu.HBM)
    dma = pltpu.SemaphoreType.DMA
    return pl.pallas_call(
        kernel,
        out_shape=jax.ShapeDtypeStruct(queries.shape, jnp.bfloat16),
        in_specs=[
            anywhere,
            anywhere,
            anywhere,
            anywhere,
            anywhere,
        ],
        out_specs=anywhere,
        scratch_shapes=[
            pltpu.VMEM((PEERS, ROWS, DIM), jnp.bfloat16),
            pltpu.VMEM((2 * PEERS, ROWS, DIM), jnp.bfloat16),
            pltpu.VMEM((2 * PEERS, ROWS, DIM), jnp.bfloat16),
            pltpu.VMEM((4 * TL, TILE, DIM), jnp.bfloat16),
            pltpu.VMEM((4 * TL, DIM + 16, TILE), jnp.bfloat16),
            pltpu.VMEM((PEERS, ROWS, DIM), jnp.bfloat16),
            pltpu.VMEM((2, WIN * TILE, 2 * TILE), jnp.float32),
            pltpu.VMEM((2, TL, WIN), jnp.int32),
            pltpu.SMEM((2, TL, WIN), jnp.int32),
            pltpu.SMEM((32 * TL,), jnp.int32),
            dma((3, PEERS)),
            dma((3, PEERS)),
            dma((2, PEERS)),
            dma((2, PEERS)),
            dma((PEERS,)),
            dma((PEERS,)),
            dma((2,)),
            dma((2,)),
            dma((2,)),
        ],
        compiler_params=pltpu.CompilerParams(
            collective_id=0, has_side_effects=True, vmem_limit_bytes=60 * 1024 * 1024
        ),
        name="tile_attention",
    )(queries, keys, values, windows, counts)


def solution(mesh):
    tokens = P(("frame", "head"), None)
    return jax.shard_map(
        shards,
        mesh=mesh,
        in_specs=(tokens, tokens, tokens, P("frame", None), P()),
        out_specs=tokens,
        check_vma=False,
    )
```

```python
import math

import jax
import jax.numpy as jnp
from jax import lax
from jax.experimental import pallas as pl
from jax.experimental.pallas import tpu as pltpu
from jax.sharding import PartitionSpec as P

HEADS = 16
DIM = 128
TILE = 128
WIN = 27
TL = 16
PEERS = 16
ROWS = 256
PART = 5
SCALE = math.log2(math.e) / math.sqrt(DIM)
KFAR, QFAR = True, False
MESH = pl.DeviceIdType.MESH


def div(a, b):
    return lax.div(a, jnp.int32(b))


def rem(a, b):
    return lax.rem(a, jnp.int32(b))


def owner(pair, head):
    z, b = div(head, 2), rem(head, 2)
    zh = div(z, 2)
    x = 2 * b + rem(div(pair, 2) + div(pair, 4) + zh, 2)
    return (div(pair, 4) * 2 + rem(z, 2)) * 4 + x, zh * 2 + rem(pair, 2)


def spread(k):
    return div(k + 1, 2) * (2 * rem(k, 2) - 1)


def kernel(
    q_ref, k_ref, v_ref, win_ref, counts_hbm, out_ref,
    qbuf, kraw, vraw, keys, vals, obuf, scores, wdst, wsm, counts_ref,
    in_send, in_recv, halo_send, halo_recv, o_send, o_recv, w_send, w_recv, local,
):
    f, hi = lax.axis_index("frame"), lax.axis_index("head")
    zl, x = rem(div(f, 4), 2), rem(f, 4)
    zh, core = div(hi, 2), rem(hi, 2)
    src_pair = div(f, 2)
    my_slot = rem(f, 2) * 8 + hi
    my_z = zh * 2 + zl
    head = 2 * my_z + div(x, 2)
    pair = div(f, 8) * 4 + rem(x + zh + div(f, 8), 2) * 2 + core
    last_pair = lax.axis_size("frame") // 2 - 1
    has_left, has_right = pair > 0, pair < last_pair
    left = owner(jnp.maximum(pair - 1, 0), head)
    right = owner(jnp.minimum(pair + 1, last_pair), head)

    def is_me(dev):
        return (dev[0] == f) & (dev[1] == hi)

    sign = 1 - 2 * core

    def dest_head(i, side, far):
        k = div(i, 2)
        z = rem(my_z + side * spread(7 - k if far else k) + 8, 8)
        return 2 * z + rem(i, 2)

    apart = rem(rem(div(pair, 2), 2) + zl, 2)
    turn = apart * (2 * zl - 1) + (1 - apart) * sign

    def source_slot(i, far):
        r = rem(i, 4)
        k = div(i, 4)
        z = rem(zh + turn * spread(3 - k if far else k) + 4, 4)
        return rem(r, 2) * 8 + z * 2 + rem(div(r, 2) + core + zl, 2)

    def source_dev(slot):
        return 2 * pair + div(slot, 8), rem(slot, 8)

    barrier = pltpu.get_barrier_semaphore()

    def greet(dev, when):
        @pl.when(when)
        def _():
            pl.semaphore_signal(barrier, inc=1, device_id=dev, device_id_type=MESH)

    def greet_step(i, carry):
        src = source_dev(i)
        greet(src, jnp.logical_not(is_me(src)))
        return carry

    counts_copy = pltpu.make_async_copy(counts_hbm, counts_ref, local.at[0])
    counts_copy.start()
    lax.fori_loop(0, PEERS, greet_step, 0)
    greet(left, has_left)
    greet(right, has_right)
    selfish = (div(f, 2) == pair).astype(jnp.int32)
    pl.semaphore_wait(
        barrier, 16 - selfish + has_left.astype(jnp.int32) + has_right.astype(jnp.int32)
    )

    def send(a, src_ref, dst_ref, h):
        dst = owner(src_pair, h)
        src = src_ref.at[:, pl.ds(pl.multiple_of(h * DIM, DIM), DIM)]
        mine = is_me(dst)

        @pl.when(jnp.logical_not(mine))
        def _():
            pltpu.make_async_remote_copy(
                src_ref=src, dst_ref=dst_ref, send_sem=in_send.at[a, h],
                recv_sem=in_recv.at[a, my_slot], device_id=dst, device_id_type=MESH,
            ).start()

        @pl.when(mine)
        def _():
            pltpu.make_async_copy(src, dst_ref, in_recv.at[a, my_slot]).start()

    def sends(i, carry):
        send(0, k_ref, kraw.at[8 + my_slot], dest_head(i, sign, KFAR))
        send(1, v_ref, vraw.at[8 + my_slot], dest_head(i, -sign, KFAR))
        return carry

    def window_send(b, start):
        h = 2 * hi + b
        dst = owner(src_pair, h)
        mine = is_me(dst)
        there = wdst.at[rem(f, 2)]

        @pl.when(jnp.logical_not(mine))
        def _():
            copy = pltpu.make_async_remote_copy(
                src_ref=win_ref, dst_ref=there, send_sem=w_send.at[b],
                recv_sem=w_recv.at[rem(f, 2)], device_id=dst, device_id_type=MESH,
            )
            if start:
                copy.start()
            else:
                copy.wait_send()

        if start:

            @pl.when(mine)
            def _():
                pltpu.make_async_copy(win_ref, there, w_recv.at[rem(f, 2)]).start()

    for b in range(2):
        window_send(b, True)
    lax.fori_loop(0, PEERS, sends, 0)

    first_tile = (2 * pair - 1) * TL
    slots = lax.broadcasted_iota(jnp.int32, (16, TILE), 1)
    row_ids = lax.broadcasted_iota(jnp.int32, (TILE, DIM), 0)

    def prepare(r):
        for u in range(2):
            count = counts_ref[first_tile + 2 * r + u]
            usable = row_ids < count
            k = kraw[r, u * TILE : (u + 1) * TILE, :].astype(jnp.float32)
            keys[2 * r + u] = jnp.where(usable, k, k[0:1, :]).astype(jnp.bfloat16)
            v = vraw[r, u * TILE : (u + 1) * TILE, :].astype(jnp.float32)
            vals[2 * r + u, 0:DIM, :] = jnp.where(usable, v, 0.0).T.astype(jnp.bfloat16)
            vals[2 * r + u, DIM:, :] = jnp.where(slots < count, 1.0, 0.0).astype(jnp.bfloat16)

    def halo(a, raw, slot, dev, there):
        return pltpu.make_async_remote_copy(
            src_ref=raw.at[8 + slot], dst_ref=raw.at[there], send_sem=halo_send.at[a, slot],
            recv_sem=halo_recv.at[a, slot], device_id=dev, device_id_type=MESH,
        )

    def arrivals(i, carry):
        slot = source_slot(i, KFAR)
        for a, raw in ((0, kraw), (1, vraw)):
            here = raw.at[8 + slot]
            pltpu.make_async_copy(here, here, in_recv.at[a, slot]).wait()

            @pl.when((slot < 8) & has_left)
            def _():
                halo(a, raw, slot, left, 24 + rem(slot, 8)).start()

            @pl.when((slot >= 8) & has_right)
            def _():
                halo(a, raw, slot, right, rem(slot, 8)).start()


        @pl.when(i >= 8)
        def _():
            for n in range(2):
                send(2, q_ref, qbuf.at[my_slot], dest_head((i - 8) * 2 + n, sign, QFAR))

        prepare(8 + slot)
        return carry

    for half in range(2):
        here = wdst.at[half]
        pltpu.make_async_copy(here, here, w_recv.at[half]).wait()
    copy = pltpu.make_async_copy(wdst, wsm, local.at[1])
    copy.start()
    copy.wait()

    def place_row(i, carry):
        half, row = div(i, TL), rem(i, TL)
        for j in range(WIN):
            wsm[half, row, j] = jnp.clip(wsm[half, row, j] - first_tile, 0, 4 * TL - 1)
        return carry

    lax.fori_loop(0, 2 * TL, place_row, 0)
    counts_copy.wait()
    lax.fori_loop(0, PEERS, arrivals, 0)

    def halo_arrivals(i, carry):
        slot = source_slot(i, KFAR)
        from_left = slot >= 8
        r = lax.select(from_left, rem(slot, 8), 24 + rem(slot, 8))

        @pl.when((from_left & has_left) | (jnp.logical_not(from_left) & has_right))
        def _():
            for a, raw in ((0, kraw), (1, vraw)):
                here = raw.at[r]
                pltpu.make_async_copy(here, here, halo_recv.at[a, slot]).wait()
            prepare(r)

        return carry

    lax.fori_loop(0, PEERS, halo_arrivals, 0)

    def places(slot):
        half, row = div(slot, 8), 2 * rem(slot, 8)
        return [[wsm[half, row + u, j] for j in range(WIN)] for u in range(2)]

    def both(slot):
        q = [qbuf[slot, u * TILE : (u + 1) * TILE, :] for u in range(2)]
        none = jnp.zeros_like(q[0])
        return jnp.concatenate(
            [jnp.concatenate([q[0], none], axis=1), jnp.concatenate([none, q[1]], axis=1)], axis=0
        )

    def score_part(j, queries, at, b, highest):
        n = min(PART, WIN - j)
        k = jnp.concatenate(
            [jnp.concatenate([keys[at[0][j + i]], keys[at[1][j + i]]], axis=1) for i in range(n)], axis=0
        )
        s = lax.dot_general(k, queries, (((1,), (1,)), ((), ())), preferred_element_type=jnp.float32)
        scores[b, j * TILE : (j + n) * TILE, :] = s
        part = jnp.max(s.reshape(n * TILE // 8, 8, 2 * TILE), axis=0)
        return part if highest is None else jnp.maximum(highest, part)

    def value_part(j, u, at, b, highest, total):
        n = min(2, WIN - j)
        v = [vals[at[u][j + i]] for i in range(n)]
        v = v[0] if n == 1 else jnp.concatenate(v, axis=1)
        columns = slice(u * TILE, (u + 1) * TILE)
        s = scores[b, j * TILE : (j + n) * TILE, columns]
        weights = jnp.exp2((s - highest[:, columns]) * SCALE).astype(jnp.bfloat16)
        part = jnp.dot(v, weights, preferred_element_type=jnp.float32)
        return part if total is None else total + part

    def stage(now, then, b, highest):
        at_now, at_then = places(now), places(then)
        queries = both(then)
        parts = list(range(0, WIN, PART))
        steps = [(u, j) for u in range(2) for j in range(0, WIN, 2)]
        coming, done = None, 0
        for step, (u, j) in enumerate(steps):
            if done < len(parts) and done * len(steps) <= step * len(parts):
                coming = score_part(parts[done], queries, at_then, 1 - b, coming)
                done += 1
            total = value_part(j, u, at_now, b, highest, total if j else None)
            if j + 2 > WIN:
                result = total[:DIM] / total[DIM : DIM + 1]
                obuf[now, u * TILE : (u + 1) * TILE, :] = result.T.astype(jnp.bfloat16)
        return jnp.max(coming, axis=0, keepdims=True)

    def query_arrival(slot):
        here = qbuf.at[slot]
        pltpu.make_async_copy(here, here, in_recv.at[2, slot]).wait()

    columns = pl.ds(pl.multiple_of(head * DIM, DIM), DIM)

    def result_copy(slot, dev):
        return pltpu.make_async_remote_copy(
            src_ref=obuf.at[slot], dst_ref=out_ref.at[:, columns], send_sem=o_send.at[slot],
            recv_sem=o_recv.at[head], device_id=dev, device_id_type=MESH,
        )

    def sent(i):
        h = dest_head(i, sign, QFAR)

        @pl.when(jnp.logical_not(is_me(owner(src_pair, h))))
        def _():
            for a, ref in ((0, k_ref), (1, v_ref), (2, q_ref)):
                src = ref.at[:, pl.ds(pl.multiple_of(h * DIM, DIM), DIM)]
                pltpu.make_async_copy(src, src, in_send.at[a, h]).wait()

        @pl.when(((i < 8) & has_left) | ((i >= 8) & has_right))
        def _():
            for a, raw in ((0, kraw), (1, vraw)):
                there = raw.at[8 + i]
                pltpu.make_async_copy(there, there, halo_send.at[a, i]).wait()

    def chunk(i, b, highest):
        slot = source_slot(i, QFAR)
        later = jnp.minimum(i + 1, PEERS - 1)
        next_slot = source_slot(later, QFAR)

        @pl.when(later > i)
        def _():
            query_arrival(next_slot)

        highest = stage(slot, next_slot, b, highest)
        dev = source_dev(slot)
        mine = is_me(dev)

        @pl.when(jnp.logical_not(mine))
        def _():
            result_copy(slot, dev).start()

        @pl.when(mine)
        def _():
            pltpu.make_async_copy(obuf.at[slot], out_ref.at[:, columns], o_recv.at[head]).start()

        sent(i)
        return highest

    def chunks(i, highest):
        for b in range(2):
            highest = chunk(2 * i + b, b, highest)
        return highest

    first = source_slot(jnp.int32(0), QFAR)
    query_arrival(first)
    highest = None
    for j in range(0, WIN, PART):
        highest = score_part(j, both(first), places(first), 0, highest)
    lax.fori_loop(0, PEERS // 2, chunks, jnp.max(highest, axis=0, keepdims=True))

    def finish(i, carry):
        @pl.when(jnp.logical_not(is_me(source_dev(i))))
        def _():
            pltpu.make_async_copy(obuf.at[i], obuf.at[i], o_send.at[i]).wait()

        got = out_ref.at[:, pl.ds(pl.multiple_of(i * DIM, DIM), DIM)]
        pltpu.make_async_copy(got, got, o_recv.at[i]).wait()
        return carry

    lax.fori_loop(0, PEERS, finish, 0)
    for b in range(2):
        window_send(b, False)


def shards(queries, keys, values, windows, counts):
    anywhere = pl.BlockSpec(memory_space=pltpu.HBM)
    dma = pltpu.SemaphoreType.DMA
    return pl.pallas_call(
        kernel,
        out_shape=pltpu.VMEM(queries.shape, jnp.bfloat16),
        in_specs=[
            anywhere,
            anywhere,
            anywhere,
            anywhere,
            anywhere,
        ],
        out_specs=pl.BlockSpec(memory_space=pltpu.VMEM),
        scratch_shapes=[
            pltpu.VMEM((PEERS, ROWS, DIM), jnp.bfloat16),
            pltpu.VMEM((2 * PEERS, ROWS, DIM), jnp.bfloat16),
            pltpu.VMEM((2 * PEERS, ROWS, DIM), jnp.bfloat16),
            pltpu.VMEM((4 * TL, TILE, DIM), jnp.bfloat16),
            pltpu.VMEM((4 * TL, DIM + 16, TILE), jnp.bfloat16),
            pltpu.VMEM((PEERS, ROWS, DIM), jnp.bfloat16),
            pltpu.VMEM((2, WIN * TILE, 2 * TILE), jnp.float32),
            pltpu.VMEM((2, TL, WIN), jnp.int32),
            pltpu.SMEM((2, TL, WIN), jnp.int32),
            pltpu.SMEM((32 * TL,), jnp.int32),
            dma((3, PEERS)),
            dma((3, PEERS)),
            dma((2, PEERS)),
            dma((2, PEERS)),
            dma((PEERS,)),
            dma((PEERS,)),
            dma((2,)),
            dma((2,)),
            dma((2,)),
        ],
        compiler_params=pltpu.CompilerParams(
            collective_id=0, has_side_effects=True, vmem_limit_bytes=60 * 1024 * 1024
        ),
        name="tile_attention",
    )(queries, keys, values, windows, counts)


def solution(mesh):
    tokens = P(("frame", "head"), None)
    return jax.shard_map(
        shards,
        mesh=mesh,
        in_specs=(tokens, tokens, tokens, P("frame", None), P()),
        out_specs=tokens,
        check_vma=False,
    )
```

```python
import math

import jax
import jax.numpy as jnp
from jax import lax
from jax.experimental import pallas as pl
from jax.experimental.pallas import tpu as pltpu
from jax.sharding import PartitionSpec as P

HEADS = 16
DIM = 128
TILE = 128
WIN = 27
TL = 16
PEERS = 16
ROWS = 256
PART = 5
SCALE = math.log2(math.e) / math.sqrt(DIM)
KFAR, QFAR = True, False
MESH = pl.DeviceIdType.MESH


def div(a, b):
    return lax.div(a, jnp.int32(b))


def rem(a, b):
    return lax.rem(a, jnp.int32(b))


def owner(pair, head):
    z, b = div(head, 2), rem(head, 2)
    zh = div(z, 2)
    x = 2 * b + rem(div(pair, 2) + div(pair, 4) + zh, 2)
    return (div(pair, 4) * 2 + rem(z, 2)) * 4 + x, zh * 2 + rem(pair, 2)


def spread(k):
    return div(k + 1, 2) * (2 * rem(k, 2) - 1)


def kernel(
    q_ref, k_ref, v_ref, win_ref, counts_hbm, out_ref,
    qbuf, kraw, vraw, keys, vals, obuf, scores, wdst, wsm, counts_ref,
    in_send, in_recv, halo_send, halo_recv, o_send, o_recv, w_send, w_recv, local,
):
    f, hi = lax.axis_index("frame"), lax.axis_index("head")
    zl, x = rem(div(f, 4), 2), rem(f, 4)
    zh, core = div(hi, 2), rem(hi, 2)
    src_pair = div(f, 2)
    my_slot = rem(f, 2) * 8 + hi
    my_z = zh * 2 + zl
    head = 2 * my_z + div(x, 2)
    pair = div(f, 8) * 4 + rem(x + zh + div(f, 8), 2) * 2 + core
    last_pair = lax.axis_size("frame") // 2 - 1
    has_left, has_right = pair > 0, pair < last_pair
    left = owner(jnp.maximum(pair - 1, 0), head)
    right = owner(jnp.minimum(pair + 1, last_pair), head)

    def is_me(dev):
        return (dev[0] == f) & (dev[1] == hi)

    sign = 1 - 2 * core

    def dest_head(i, side, far):
        k = div(i, 2)
        z = rem(my_z + side * spread(7 - k if far else k) + 8, 8)
        return 2 * z + rem(i, 2)

    apart = rem(rem(div(pair, 2), 2) + zl, 2)
    turn = apart * (2 * zl - 1) + (1 - apart) * sign

    def source_slot(i, far):
        r = rem(i, 4)
        k = div(i, 4)
        z = rem(zh + turn * spread(3 - k if far else k) + 4, 4)
        return rem(r, 2) * 8 + z * 2 + rem(div(r, 2) + core + zl, 2)

    def source_dev(slot):
        return 2 * pair + div(slot, 8), rem(slot, 8)

    barrier = pltpu.get_barrier_semaphore()

    def greet(dev, when):
        @pl.when(when)
        def _():
            pl.semaphore_signal(barrier, inc=1, device_id=dev, device_id_type=MESH)

    def greet_step(i, carry):
        src = source_dev(i)
        greet(src, jnp.logical_not(is_me(src)))
        return carry

    counts_copy = pltpu.make_async_copy(counts_hbm, counts_ref, local.at[0])
    counts_copy.start()
    lax.fori_loop(0, PEERS, greet_step, 0)
    greet(left, has_left)
    greet(right, has_right)
    selfish = (div(f, 2) == pair).astype(jnp.int32)
    pl.semaphore_wait(
        barrier, 16 - selfish + has_left.astype(jnp.int32) + has_right.astype(jnp.int32)
    )

    def send(a, src_ref, dst_ref, h):
        dst = owner(src_pair, h)
        src = src_ref.at[:, pl.ds(pl.multiple_of(h * DIM, DIM), DIM)]
        mine = is_me(dst)

        @pl.when(jnp.logical_not(mine))
        def _():
            pltpu.make_async_remote_copy(
                src_ref=src, dst_ref=dst_ref, send_sem=in_send.at[a, h],
                recv_sem=in_recv.at[a, my_slot], device_id=dst, device_id_type=MESH,
            ).start()

        @pl.when(mine)
        def _():
            pltpu.make_async_copy(src, dst_ref, in_recv.at[a, my_slot]).start()

    def sends(i, carry):
        send(0, k_ref, kraw.at[8 + my_slot], dest_head(rem(i + 8 * core, 16), sign, KFAR))
        send(1, v_ref, vraw.at[8 + my_slot], dest_head(rem(i + 8 * core, 16), -sign, KFAR))
        return carry

    def window_send(b, start):
        h = 2 * hi + b
        dst = owner(src_pair, h)
        mine = is_me(dst)
        there = wdst.at[rem(f, 2)]

        @pl.when(jnp.logical_not(mine))
        def _():
            copy = pltpu.make_async_remote_copy(
                src_ref=win_ref, dst_ref=there, send_sem=w_send.at[b],
                recv_sem=w_recv.at[rem(f, 2)], device_id=dst, device_id_type=MESH,
            )
            if start:
                copy.start()
            else:
                copy.wait_send()

        if start:

            @pl.when(mine)
            def _():
                pltpu.make_async_copy(win_ref, there, w_recv.at[rem(f, 2)]).start()

    for b in range(2):
        window_send(b, True)
    lax.fori_loop(0, PEERS, sends, 0)

    first_tile = (2 * pair - 1) * TL
    slots = lax.broadcasted_iota(jnp.int32, (16, TILE), 1)
    row_ids = lax.broadcasted_iota(jnp.int32, (TILE, DIM), 0)

    def prepare(r):
        for u in range(2):
            count = counts_ref[first_tile + 2 * r + u]
            usable = row_ids < count
            k = kraw[r, u * TILE : (u + 1) * TILE, :].astype(jnp.float32)
            keys[2 * r + u] = jnp.where(usable, k, k[0:1, :]).astype(jnp.bfloat16)
            v = vraw[r, u * TILE : (u + 1) * TILE, :].astype(jnp.float32)
            vals[2 * r + u, 0:DIM, :] = jnp.where(usable, v, 0.0).T.astype(jnp.bfloat16)
            vals[2 * r + u, DIM:, :] = jnp.where(slots < count, 1.0, 0.0).astype(jnp.bfloat16)

    def halo(a, raw, slot, dev, there):
        return pltpu.make_async_remote_copy(
            src_ref=raw.at[8 + slot], dst_ref=raw.at[there], send_sem=halo_send.at[a, slot],
            recv_sem=halo_recv.at[a, slot], device_id=dev, device_id_type=MESH,
        )

    def arrivals(i, carry):
        slot = source_slot(i, KFAR)
        for a, raw in ((0, kraw), (1, vraw)):
            here = raw.at[8 + slot]
            pltpu.make_async_copy(here, here, in_recv.at[a, slot]).wait()

            @pl.when((slot < 8) & has_left)
            def _():
                halo(a, raw, slot, left, 24 + rem(slot, 8)).start()

            @pl.when((slot >= 8) & has_right)
            def _():
                halo(a, raw, slot, right, rem(slot, 8)).start()


        @pl.when(i >= 8)
        def _():
            for n in range(2):
                send(2, q_ref, qbuf.at[my_slot], dest_head((i - 8) * 2 + n, sign, QFAR))

        prepare(8 + slot)
        return carry

    for half in range(2):
        here = wdst.at[half]
        pltpu.make_async_copy(here, here, w_recv.at[half]).wait()
    copy = pltpu.make_async_copy(wdst, wsm, local.at[1])
    copy.start()
    copy.wait()

    def place_row(i, carry):
        half, row = div(i, TL), rem(i, TL)
        for j in range(WIN):
            wsm[half, row, j] = jnp.clip(wsm[half, row, j] - first_tile, 0, 4 * TL - 1)
        return carry

    lax.fori_loop(0, 2 * TL, place_row, 0)
    counts_copy.wait()
    lax.fori_loop(0, PEERS, arrivals, 0)

    def halo_arrivals(i, carry):
        slot = source_slot(i, KFAR)
        from_left = slot >= 8
        r = lax.select(from_left, rem(slot, 8), 24 + rem(slot, 8))

        @pl.when((from_left & has_left) | (jnp.logical_not(from_left) & has_right))
        def _():
            for a, raw in ((0, kraw), (1, vraw)):
                here = raw.at[r]
                pltpu.make_async_copy(here, here, halo_recv.at[a, slot]).wait()
            prepare(r)

        return carry

    lax.fori_loop(0, PEERS, halo_arrivals, 0)

    def places(slot):
        half, row = div(slot, 8), 2 * rem(slot, 8)
        return [[wsm[half, row + u, j] for j in range(WIN)] for u in range(2)]

    def both(slot):
        q = [qbuf[slot, u * TILE : (u + 1) * TILE, :] for u in range(2)]
        none = jnp.zeros_like(q[0])
        return jnp.concatenate(
            [jnp.concatenate([q[0], none], axis=1), jnp.concatenate([none, q[1]], axis=1)], axis=0
        )

    def score_part(j, queries, at, b, highest):
        n = min(PART, WIN - j)
        k = jnp.concatenate(
            [jnp.concatenate([keys[at[0][j + i]], keys[at[1][j + i]]], axis=1) for i in range(n)], axis=0
        )
        s = lax.dot_general(k, queries, (((1,), (1,)), ((), ())), preferred_element_type=jnp.float32)
        scores[b, j * TILE : (j + n) * TILE, :] = s
        part = jnp.max(s.reshape(n * TILE // 8, 8, 2 * TILE), axis=0)
        return part if highest is None else jnp.maximum(highest, part)

    def value_part(j, u, at, b, highest, total):
        n = min(2, WIN - j)
        v = [vals[at[u][j + i]] for i in range(n)]
        v = v[0] if n == 1 else jnp.concatenate(v, axis=1)
        columns = slice(u * TILE, (u + 1) * TILE)
        s = scores[b, j * TILE : (j + n) * TILE, columns]
        weights = jnp.exp2((s - highest[:, columns]) * SCALE).astype(jnp.bfloat16)
        part = jnp.dot(v, weights, preferred_element_type=jnp.float32)
        return part if total is None else total + part

    def stage(now, then, b, highest):
        at_now, at_then = places(now), places(then)
        queries = both(then)
        parts = list(range(0, WIN, PART))
        steps = [(u, j) for u in range(2) for j in range(0, WIN, 2)]
        coming, done = None, 0
        for step, (u, j) in enumerate(steps):
            if done < len(parts) and done * len(steps) <= step * len(parts):
                coming = score_part(parts[done], queries, at_then, 1 - b, coming)
                done += 1
            total = value_part(j, u, at_now, b, highest, total if j else None)
            if j + 2 > WIN:
                result = total[:DIM] / total[DIM : DIM + 1]
                obuf[now, u * TILE : (u + 1) * TILE, :] = result.T.astype(jnp.bfloat16)
        return jnp.max(coming, axis=0, keepdims=True)

    def query_arrival(slot):
        here = qbuf.at[slot]
        pltpu.make_async_copy(here, here, in_recv.at[2, slot]).wait()

    columns = pl.ds(pl.multiple_of(head * DIM, DIM), DIM)

    def result_copy(slot, dev):
        return pltpu.make_async_remote_copy(
            src_ref=obuf.at[slot], dst_ref=out_ref.at[:, columns], send_sem=o_send.at[slot],
            recv_sem=o_recv.at[head], device_id=dev, device_id_type=MESH,
        )

    def sent(i):
        h = dest_head(i, sign, QFAR)

        @pl.when(jnp.logical_not(is_me(owner(src_pair, h))))
        def _():
            for a, ref in ((0, k_ref), (1, v_ref), (2, q_ref)):
                src = ref.at[:, pl.ds(pl.multiple_of(h * DIM, DIM), DIM)]
                pltpu.make_async_copy(src, src, in_send.at[a, h]).wait()

        @pl.when(((i < 8) & has_left) | ((i >= 8) & has_right))
        def _():
            for a, raw in ((0, kraw), (1, vraw)):
                there = raw.at[8 + i]
                pltpu.make_async_copy(there, there, halo_send.at[a, i]).wait()

    def chunk(i, b, highest):
        slot = source_slot(i, QFAR)
        later = jnp.minimum(i + 1, PEERS - 1)
        next_slot = source_slot(later, QFAR)

        @pl.when(later > i)
        def _():
            query_arrival(next_slot)

        highest = stage(slot, next_slot, b, highest)
        dev = source_dev(slot)
        mine = is_me(dev)

        @pl.when(jnp.logical_not(mine))
        def _():
            result_copy(slot, dev).start()

        @pl.when(mine)
        def _():
            pltpu.make_async_copy(obuf.at[slot], out_ref.at[:, columns], o_recv.at[head]).start()

        sent(i)
        return highest

    def chunks(i, highest):
        for b in range(2):
            highest = chunk(2 * i + b, b, highest)
        return highest

    first = source_slot(jnp.int32(0), QFAR)
    query_arrival(first)
    highest = None
    for j in range(0, WIN, PART):
        highest = score_part(j, both(first), places(first), 0, highest)
    lax.fori_loop(0, PEERS // 2, chunks, jnp.max(highest, axis=0, keepdims=True))

    def finish(i, carry):
        @pl.when(jnp.logical_not(is_me(source_dev(i))))
        def _():
            pltpu.make_async_copy(obuf.at[i], obuf.at[i], o_send.at[i]).wait()

        got = out_ref.at[:, pl.ds(pl.multiple_of(i * DIM, DIM), DIM)]
        pltpu.make_async_copy(got, got, o_recv.at[i]).wait()
        return carry

    lax.fori_loop(0, PEERS, finish, 0)
    for b in range(2):
        window_send(b, False)


def shards(queries, keys, values, windows, counts):
    anywhere = pl.BlockSpec(memory_space=pltpu.HBM)
    dma = pltpu.SemaphoreType.DMA
    return pl.pallas_call(
        kernel,
        out_shape=pltpu.VMEM(queries.shape, jnp.bfloat16),
        in_specs=[
            anywhere,
            anywhere,
            anywhere,
            anywhere,
            anywhere,
        ],
        out_specs=pl.BlockSpec(memory_space=pltpu.VMEM),
        scratch_shapes=[
            pltpu.VMEM((PEERS, ROWS, DIM), jnp.bfloat16),
            pltpu.VMEM((2 * PEERS, ROWS, DIM), jnp.bfloat16),
            pltpu.VMEM((2 * PEERS, ROWS, DIM), jnp.bfloat16),
            pltpu.VMEM((4 * TL, TILE, DIM), jnp.bfloat16),
            pltpu.VMEM((4 * TL, DIM + 16, TILE), jnp.bfloat16),
            pltpu.VMEM((PEERS, ROWS, DIM), jnp.bfloat16),
            pltpu.VMEM((2, WIN * TILE, 2 * TILE), jnp.float32),
            pltpu.VMEM((2, TL, WIN), jnp.int32),
            pltpu.SMEM((2, TL, WIN), jnp.int32),
            pltpu.SMEM((32 * TL,), jnp.int32),
            dma((3, PEERS)),
            dma((3, PEERS)),
            dma((2, PEERS)),
            dma((2, PEERS)),
            dma((PEERS,)),
            dma((PEERS,)),
            dma((2,)),
            dma((2,)),
            dma((2,)),
        ],
        compiler_params=pltpu.CompilerParams(
            collective_id=0, has_side_effects=True, vmem_limit_bytes=60 * 1024 * 1024
        ),
        name="tile_attention",
    )(queries, keys, values, windows, counts)


def solution(mesh):
    tokens = P(("frame", "head"), None)
    return jax.shard_map(
        shards,
        mesh=mesh,
        in_specs=(tokens, tokens, tokens, P("frame", None), P()),
        out_specs=tokens,
        check_vma=False,
    )
```
